512 devices in a mesh: row: 8 (over y), col: 16 (over z, core), rep: 4 (over x).
Axes of the slice: x: 4, y: 8, z: 8, core: 2. Of those that a mesh axis runs over, the one named last changes fastest.
Arguments:
- a_blocks: bfloat16 [128, 128, 64, 128], P('row', ('col', 'rep')), may hold values from -0.0014648438 to 0.0014648438
- a_pattern: int32 [128, 128], P('row', ('col', 'rep')), may hold values 0 or 1
- p_blocks: bfloat16 [128, 32, 64, 128], P('row', 'col'), may hold values from -6 to 6
- p_pattern: int32 [128, 32], P('row', 'col'), may hold values 0 or 1
Outputs:
- coarse: float32 [32, 32, 64, 128], P(('row', 'rep'), 'col')
The draws below stay inside these ranges and needn't reach their ends.
All inputs are finite; a program needn't handle non-finite values. No bound on the sum of `a_pattern` or of `p_pattern` on one device may be relied on, other than what follows from the above.
Results may differ from the reference program's by a relative error of at most 0.0029.
Values may be sent and summed in bfloat16 or wider, within the bound.
No kernel may reach another device: no remote copies, remote signals or barrier semaphores. Data moves between devices by JAX's collectives and lax.ppermute only.
A program may use at most 64 MiB of HBM per device.

```python
import jax
import jax.numpy as jnp
from jax import lax

BLOCK = 64
NF = 128
NK = 32


def touch_ends(values, key, least, largest):
    longest = values.shape.index(max(values.shape))
    spots = []
    for shift in (0, 1):
        where = [jax.random.randint(jax.random.fold_in(key, axis), (), 0, length) for axis, length in enumerate(values.shape)]
        where[longest] = (where[longest] + shift) % values.shape[longest]
        spots.append(tuple(where))
    return values.at[spots[0]].set(least).at[spots[1]].set(largest)


def block_levels(own_key, extent, cuts, least, high):
    gain = 1.0
    for axis_at, blocks in cuts:
        steps = jax.random.uniform(jax.random.fold_in(jax.random.fold_in(own_key, 6), axis_at), (blocks,), jnp.float32, least / len(cuts), high / len(cuts))
        gain = gain * jnp.repeat(jnp.exp(steps), extent[axis_at] // blocks).reshape((-1,) + (1,) * (len(extent) - 1 - axis_at))
    return gain


def scatter_about(rng, shape, spread, reach, shards=(), held_as=jnp.bfloat16):
    values = jax.random.normal(rng, shape, jnp.float32) * spread
    if len(shards) > 0:
        values = block_levels(rng, shape, shards, -0.22, 0.18) * values
    return jnp.clip(values, min=-reach, max=reach).astype(held_as)


def setup_inputs(seed: int = 0) -> dict:
    arg_keys = jax.random.split(jax.random.key(seed), 5)
    return {
        "a_blocks": scatter_about(arg_keys[0], (NF, NF, BLOCK, 2 * BLOCK), (NF * NF * BLOCK * BLOCK // 4) ** -0.5, 0.0014648438, ((0, 8), (1, 64))),
        "a_pattern": touch_ends((jax.random.randint(arg_keys[1], (NF, NF), 0, 2) < 1).astype(jnp.int32), jax.random.fold_in(arg_keys[1], 1), 0, 1),
        "p_blocks": scatter_about(arg_keys[2], (NF, NK, BLOCK, 2 * BLOCK), 1.0, 6.0, ((0, 8), (1, 16))),
        "p_pattern": touch_ends((jax.random.randint(arg_keys[3], (NF, NK), 0, 2) < 1).astype(jnp.int32), jax.random.fold_in(arg_keys[3], 1), 0, 1),
    }


def real_form(blocks):
    half = blocks.shape[-1] // 2
    lower = jnp.concatenate([-blocks[..., half:], blocks[..., :half]], axis=-1)
    return jnp.concatenate([blocks, lower], axis=-2)


def transposed(blocks):
    order = blocks.shape[-2]
    lead = blocks.shape[:-2]
    split = blocks.reshape(lead + (order, 2, order))
    moved = jnp.swapaxes(split, -3, -1)
    return moved.reshape(lead + (order, 2 * order))


def flatten_right(blocks):
    count, width, deep, wide = blocks.shape
    return jnp.transpose(blocks, (0, 2, 1, 3)).reshape((count * deep, width * wide))


def reference(a_blocks, a_pattern, p_blocks, p_pattern):
    a_live = jnp.where(a_pattern[:, :, None, None] > 0, a_blocks, jnp.zeros_like(a_blocks))
    p_live = jnp.where(p_pattern[:, :, None, None] > 0, p_blocks, jnp.zeros_like(p_blocks))
    fine = p_live.shape[0]
    coarse_count = p_live.shape[1]
    order = p_live.shape[2]
    right_first = flatten_right(real_form(p_live))

    def row_product(a_row):
        left = jnp.transpose(a_row, (1, 0, 2)).reshape((order, fine * 2 * order))
        result = jnp.dot(left, right_first, preferred_element_type=jnp.float32)
        return jnp.transpose(result.reshape((order, coarse_count, 2 * order)), (1, 0, 2))

    product = lax.map(row_product, a_live).astype(jnp.bfloat16)
    right_second = flatten_right(real_form(product))
    left_blocks = jnp.swapaxes(transposed(p_live), 0, 1)

    def coarse_row(column):
        left = jnp.transpose(column, (1, 0, 2)).reshape((order, fine * 2 * order))
        result = jnp.dot(left, right_second, preferred_element_type=jnp.float32)
        return jnp.transpose(result.reshape((order, coarse_count, 2 * order)), (1, 0, 2))

    return lax.map(coarse_row, left_blocks)
```

```python
import functools

import jax
import jax.numpy as jnp
from jax import lax
from jax.experimental import pallas as pl
from jax.experimental.pallas import tpu as pltpu
from jax.sharding import Mesh, PartitionSpec as P

BLOCK = 64
BF16 = jnp.bfloat16
F32 = jnp.float32


def lower_half(block):
    lane = lax.broadcasted_iota(jnp.int32, block.shape, block.ndim - 1)
    turned = jnp.concatenate([block[..., BLOCK:], block[..., :BLOCK]], axis=-1)
    return jnp.where(lane < BLOCK, -turned, turned)


def real_pair(blocks):
    return jnp.concatenate([jnp.concatenate([b, lower_half(b)], axis=0) for b in blocks], axis=1)


def product_kernel(a_ref, p_ref, out_ref):
    step = pl.program_id(0)
    rows = a_ref.shape[1]
    left = jnp.concatenate(
        [a_ref[0, :, e].reshape(rows * BLOCK, 2 * BLOCK) for e in range(2)], axis=1
    )
    right = jnp.concatenate([real_pair([p_ref[0, e, 0], p_ref[0, e, 1]]) for e in range(2)], axis=0)
    term = jnp.dot(left, right, preferred_element_type=F32)
    for b in range(2):
        part = term[:, b * 2 * BLOCK : (b + 1) * 2 * BLOCK].reshape(rows, BLOCK, 2 * BLOCK)

        @pl.when(step == 0)
        def _():
            out_ref[:, b] = part

        @pl.when(step > 0)
        def _():
            out_ref[:, b] += part


def partial_product(a_all, p_all):
    steps, rows = a_all.shape[0], a_all.shape[1]
    return pl.pallas_call(
        product_kernel,
        grid=(steps,),
        in_specs=[
            pl.BlockSpec((1, rows, 2, BLOCK, 2 * BLOCK), lambda s: (s, 0, 0, 0, 0)),
            pl.BlockSpec((1, 2, 2, BLOCK, 2 * BLOCK), lambda s: (s, 0, 0, 0, 0)),
        ],
        out_specs=pl.BlockSpec((rows, 2, BLOCK, 2 * BLOCK), lambda s: (0, 0, 0, 0)),
        out_shape=jax.ShapeDtypeStruct((rows, 2, BLOCK, 2 * BLOCK), F32),
        name="product_terms",
    )(a_all, p_all)


def sum_kernel(copies, in_ref, out_ref):
    total = in_ref[0]
    for s in range(1, in_ref.shape[0]):
        total = total + in_ref[s]
    rounded = total.astype(BF16)
    for c in range(copies):
        out_ref[c] = rounded


def coarse_kernel(left_ref, prod_ref, out_ref):
    groups = left_ref.shape[0]
    total = jnp.zeros((groups * BLOCK, 4 * BLOCK), F32)
    for i in range(0, prod_ref.shape[0], 2):
        left = jnp.concatenate(
            [
                left_ref[:, (i + e) // 8, (i + e) % 8].reshape(groups * BLOCK, 2 * BLOCK)
                for e in range(2)
            ],
            axis=1,
        )
        right = jnp.concatenate(
            [real_pair([prod_ref[i + e, 0], prod_ref[i + e, 1]]) for e in range(2)], axis=0
        )
        total = total + jnp.dot(left, right, preferred_element_type=F32)
    for b in range(2):
        out_ref[:, b] = (
            total[:, b * 2 * BLOCK : (b + 1) * 2 * BLOCK]
            .reshape(groups, BLOCK, 2 * BLOCK)
            .astype(BF16)
        )


def final_kernel(in_ref, out_ref):
    total = in_ref[0].astype(F32)
    for s in range(1, in_ref.shape[0]):
        total = total + in_ref[s].astype(F32)
    out_ref[0] = total


def call(kernel, out_shape, *args):
    return pl.pallas_call(
        kernel,
        out_shape=out_shape,
        in_specs=[pl.BlockSpec(memory_space=pltpu.VMEM)] * len(args),
        out_specs=pl.BlockSpec(memory_space=pltpu.VMEM),
        compiler_params=pltpu.CompilerParams(vmem_limit_bytes=32 * 1024 * 1024),
    )(*args)


def transposed(blocks):
    lead = blocks.shape[:-2]
    split = blocks.reshape(lead + (BLOCK, 2, BLOCK))
    return jnp.swapaxes(split, -3, -1).reshape(lead + (BLOCK, 2 * BLOCK))


def per_device(a_blocks, a_pattern, p_blocks, p_pattern):
    x = lax.axis_index("rep")
    core = lax.axis_index("core")
    layers, rings = lax.axis_size("rep"), lax.axis_size("row")
    a_live = jnp.where(a_pattern[:, :, None, None] > 0, a_blocks, jnp.zeros_like(a_blocks))
    a_all = lax.all_gather(a_live, ("z", "core"), axis=0, tiled=False)
    p_live = jnp.where(p_pattern[:, :, None, None] > 0, p_blocks, jnp.zeros_like(p_blocks))

    mine = lax.dynamic_slice_in_dim(
        p_live.reshape(2, 4, 2, 2, BLOCK, 2 * BLOCK), x, 1, axis=1
    ).reshape(1, 2, 2, 2, BLOCK, 2 * BLOCK)
    met = lax.all_to_all(
        jnp.broadcast_to(mine, (rings,) + mine.shape[1:]), "row", 0, 0, tiled=True
    )

    column = lax.dynamic_index_in_dim(p_live, x % 2, axis=1, keepdims=False)
    column = transposed(column).reshape(2, 8, BLOCK, 2 * BLOCK)
    own = lax.dynamic_index_in_dim(column, core, axis=0, keepdims=False)
    other = lax.dynamic_index_in_dim(column, 1 - core, axis=0, keepdims=False)
    got = lax.ppermute(other, "core", [(0, 1), (1, 0)])
    left = lax.all_gather(
        jnp.where(core == x // 2, own, got), ("z", "core"), axis=0, tiled=False
    ).reshape(8, 2, 8, BLOCK, 2 * BLOCK)

    terms = partial_product(a_all, met.reshape(2 * rings, 2, 2, BLOCK, 2 * BLOCK))
    swapped = lax.all_to_all(terms, "rep", 0, 0, tiled=True)
    share = terms.shape[0] // layers
    product = call(
        functools.partial(sum_kernel, layers),
        jax.ShapeDtypeStruct((layers, share, 2, BLOCK, 2 * BLOCK), BF16),
        swapped.reshape(layers, share, 2, BLOCK, 2 * BLOCK),
    )
    product = lax.all_to_all(product, "rep", 0, 0, tiled=True)
    coarse = call(
        coarse_kernel,
        jax.ShapeDtypeStruct((8, 2, BLOCK, 2 * BLOCK), BF16),
        left,
        product.reshape(layers * share, 2, BLOCK, 2 * BLOCK),
    )
    coarse = lax.all_to_all(coarse, "row", 0, 0, tiled=True)
    return call(final_kernel, jax.ShapeDtypeStruct((1, 2, BLOCK, 2 * BLOCK), F32), coarse)


def solution(mesh):
    rows, cols, reps = (mesh.shape[name] for name in ("row", "col", "rep"))
    fine = Mesh(mesh.devices.reshape(rows, cols // 2, 2, reps), ("row", "z", "core", "rep"))
    return jax.shard_map(
        per_device,
        mesh=fine,
        in_specs=(
            P("row", ("z", "core", "rep"), None, None),
            P("row", ("z", "core", "rep")),
            P("row", ("z", "core"), None, None),
            P("row", ("z", "core")),
        ),
        out_specs=P(("row", "rep"), ("z", "core"), None, None),
        check_vma=False,
    )
```

```python
import functools

import jax
import jax.numpy as jnp
from jax import lax
from jax.experimental import pallas as pl
from jax.experimental.pallas import tpu as pltpu
from jax.sharding import Mesh, PartitionSpec as P

BLOCK = 64
BF16 = jnp.bfloat16
F32 = jnp.float32


def lower_half(block):
    lane = lax.broadcasted_iota(jnp.int32, block.shape, block.ndim - 1)
    turned = jnp.concatenate([block[..., BLOCK:], block[..., :BLOCK]], axis=-1)
    return jnp.where(lane < BLOCK, -turned, turned)


def real_pair(blocks):
    return jnp.concatenate([jnp.concatenate([b, lower_half(b)], axis=0) for b in blocks], axis=1)


def product_kernel(pattern_ref, a_ref, p_ref, out_ref, right):
    groups, part = a_ref.shape[0], a_ref.shape[1]
    step, steps = pl.program_id(0), pl.num_programs(0)
    zero = jnp.zeros((BLOCK, 2 * BLOCK), BF16)

    @pl.when(step == 0)
    def _():
        for g in range(groups):
            right[g] = jnp.concatenate(
                [real_pair([p_ref[g, e, 0], p_ref[g, e, 1]]) for e in range(2)], axis=0
            )

    total = jnp.zeros((part * BLOCK, 4 * BLOCK), F32)
    for g in range(groups):
        at = (g * steps + step) * part * 2
        sides = [
            jnp.concatenate(
                [
                    jnp.where(pattern_ref[at + 2 * i + e] > 0, a_ref[g, i, e], zero)
                    for i in range(part)
                ],
                axis=0,
            )
            for e in range(2)
        ]
        total += jnp.dot(
            jnp.concatenate(sides, axis=1), right[g], preferred_element_type=F32
        )
    for b in range(2):
        out_ref[:, b] = total[:, b * 2 * BLOCK : (b + 1) * 2 * BLOCK].reshape(part, BLOCK, 2 * BLOCK)


def partial_product(pattern, a_all, p_all, part=8):
    groups, rows = a_all.shape[0], a_all.shape[1]
    block = (BLOCK, 2 * BLOCK)
    return pl.pallas_call(
        product_kernel,
        grid=(rows // part,),
        in_specs=[
            pl.BlockSpec(memory_space=pltpu.SMEM),
            pl.BlockSpec((groups, part, 2) + block, lambda s: (0, s, 0, 0, 0)),
            pl.BlockSpec((groups, 2, 2) + block, lambda s: (0, 0, 0, 0, 0)),
        ],
        out_specs=pl.BlockSpec((part, 2) + block, lambda s: (s, 0, 0, 0)),
        out_shape=jax.ShapeDtypeStruct((rows, 2) + block, F32),
        scratch_shapes=[pltpu.VMEM((groups, 4 * BLOCK, 4 * BLOCK), BF16)],
        compiler_params=pltpu.CompilerParams(vmem_limit_bytes=32 * 1024 * 1024),
        name="product_terms",
    )(pattern, a_all, p_all)


def sum_kernel(copies, in_ref, out_ref):
    total = in_ref[0]
    for s in range(1, in_ref.shape[0]):
        total = total + in_ref[s]
    rounded = total.astype(BF16)
    for c in range(copies):
        out_ref[c] = rounded


def coarse_kernel(left_ref, prod_ref, out_ref):
    groups = left_ref.shape[0]
    total = jnp.zeros((groups * BLOCK, 4 * BLOCK), F32)
    for i in range(0, prod_ref.shape[0], 2):
        left = jnp.concatenate(
            [
                left_ref[:, (i + e) // 8, (i + e) % 8].reshape(groups * BLOCK, 2 * BLOCK)
                for e in range(2)
            ],
            axis=1,
        )
        right = jnp.concatenate(
            [real_pair([prod_ref[i + e, 0], prod_ref[i + e, 1]]) for e in range(2)], axis=0
        )
        total = total + jnp.dot(left, right, preferred_element_type=F32)
    for b in range(2):
        out_ref[:, b] = (
            total[:, b * 2 * BLOCK : (b + 1) * 2 * BLOCK]
            .reshape(groups, BLOCK, 2 * BLOCK)
            .astype(BF16)
        )


def final_kernel(in_ref, out_ref):
    total = in_ref[0].astype(F32)
    for s in range(1, in_ref.shape[0]):
        total = total + in_ref[s].astype(F32)
    out_ref[0] = total


def call(kernel, out_shape, *args):
    return pl.pallas_call(
        kernel,
        out_shape=out_shape,
        in_specs=[pl.BlockSpec(memory_space=pltpu.VMEM)] * len(args),
        out_specs=pl.BlockSpec(memory_space=pltpu.VMEM),
        compiler_params=pltpu.CompilerParams(vmem_limit_bytes=32 * 1024 * 1024),
    )(*args)


def transposed(blocks):
    lead = blocks.shape[:-2]
    split = blocks.reshape(lead + (BLOCK, 2, BLOCK))
    return jnp.swapaxes(split, -3, -1).reshape(lead + (BLOCK, 2 * BLOCK))


def per_device(a_blocks, a_pattern, p_blocks, p_pattern):
    x = lax.axis_index("rep")
    core = lax.axis_index("core")
    layers, rings = lax.axis_size("rep"), lax.axis_size("row")
    a_all = lax.all_gather(a_blocks, ("z", "core"), axis=0, tiled=False)
    columns = 2 * lax.axis_size("z")
    kept = lax.all_to_all(
        jnp.broadcast_to(a_pattern[None], (columns,) + a_pattern.shape), ("z", "core"), 0, 0, tiled=True
    )
    p_live = jnp.where(p_pattern[:, :, None, None] > 0, p_blocks, jnp.zeros_like(p_blocks))

    mine = lax.dynamic_slice_in_dim(
        p_live.reshape(2, 4, 2, 2, BLOCK, 2 * BLOCK), x, 1, axis=1
    ).reshape(1, 2, 2, 2, BLOCK, 2 * BLOCK)
    met = lax.all_to_all(
        jnp.broadcast_to(mine, (rings,) + mine.shape[1:]), "row", 0, 0, tiled=True
    )

    column = lax.dynamic_index_in_dim(p_live, x % 2, axis=1, keepdims=False)
    column = transposed(column).reshape(2, 8, BLOCK, 2 * BLOCK)
    own = lax.dynamic_index_in_dim(column, core, axis=0, keepdims=False)
    other = lax.dynamic_index_in_dim(column, 1 - core, axis=0, keepdims=False)
    got = lax.ppermute(other, "core", [(0, 1), (1, 0)])
    left = lax.all_gather(
        jnp.where(core == x // 2, own, got), ("z", "core"), axis=0, tiled=False
    ).reshape(8, 2, 8, BLOCK, 2 * BLOCK)

    terms = partial_product(kept.reshape(-1), a_all, met.reshape(2 * rings, 2, 2, BLOCK, 2 * BLOCK))
    swapped = lax.all_to_all(terms, "rep", 0, 0, tiled=True)
    share = terms.shape[0] // layers
    product = call(
        functools.partial(sum_kernel, layers),
        jax.ShapeDtypeStruct((layers, share, 2, BLOCK, 2 * BLOCK), BF16),
        swapped.reshape(layers, share, 2, BLOCK, 2 * BLOCK),
    )
    product = lax.all_to_all(product, "rep", 0, 0, tiled=True)
    coarse = call(
        coarse_kernel,
        jax.ShapeDtypeStruct((8, 2, BLOCK, 2 * BLOCK), BF16),
        left,
        product.reshape(layers * share, 2, BLOCK, 2 * BLOCK),
    )
    coarse = lax.all_to_all(coarse, "row", 0, 0, tiled=True)
    return call(final_kernel, jax.ShapeDtypeStruct((1, 2, BLOCK, 2 * BLOCK), F32), coarse)


def solution(mesh):
    rows, cols, reps = (mesh.shape[name] for name in ("row", "col", "rep"))
    fine = Mesh(mesh.devices.reshape(rows, cols // 2, 2, reps), ("row", "z", "core", "rep"))
    return jax.shard_map(
        per_device,
        mesh=fine,
        in_specs=(
            P("row", ("z", "core", "rep"), None, None),
            P("row", ("z", "core", "rep")),
            P("row", ("z", "core"), None, None),
            P("row", ("z", "core")),
        ),
        out_specs=P(("row", "rep"), ("z", "core"), None, None),
        check_vma=False,
    )
```

```python
import functools

import jax
import jax.numpy as jnp
from jax import lax
from jax.experimental import pallas as pl
from jax.experimental.pallas import tpu as pltpu
from jax.sharding import Mesh, PartitionSpec as P

BLOCK = 64
BF16 = jnp.bfloat16
F32 = jnp.float32


def lower_half(block):
    lane = lax.broadcasted_iota(jnp.int32, block.shape, block.ndim - 1)
    turned = jnp.concatenate([block[..., BLOCK:], block[..., :BLOCK]], axis=-1)
    return jnp.where(lane < BLOCK, -turned, turned)


def real_pair(blocks):
    return jnp.concatenate([jnp.concatenate([b, lower_half(b)], axis=0) for b in blocks], axis=1)


def product_kernel(pattern_ref, a_ref, p_ref, out_ref, right):
    groups, part = a_ref.shape[0], a_ref.shape[1]
    step, steps = pl.program_id(0), pl.num_programs(0)
    zero = jnp.zeros((BLOCK, 2 * BLOCK), BF16)

    @pl.when(step == 0)
    def _():
        for g in range(groups):
            right[g] = jnp.concatenate(
                [real_pair([p_ref[g, e, 0], p_ref[g, e, 1]]) for e in range(2)], axis=0
            )

    total = jnp.zeros((part * BLOCK, 4 * BLOCK), F32)
    for g in range(groups):
        at = (g * steps + step) * part * 2
        sides = [
            jnp.concatenate(
                [
                    jnp.where(pattern_ref[at + 2 * i + e] > 0, a_ref[g, i, e], zero)
                    for i in range(part)
                ],
                axis=0,
            )
            for e in range(2)
        ]
        total += jnp.dot(
            jnp.concatenate(sides, axis=1), right[g], preferred_element_type=F32
        )
    for b in range(2):
        out_ref[:, b] = total[:, b * 2 * BLOCK : (b + 1) * 2 * BLOCK].reshape(part, BLOCK, 2 * BLOCK)


def partial_product(pattern, a_all, p_all, part=8):
    groups, rows = a_all.shape[0], a_all.shape[1]
    block = (BLOCK, 2 * BLOCK)
    return pl.pallas_call(
        product_kernel,
        grid=(rows // part,),
        in_specs=[
            pl.BlockSpec(memory_space=pltpu.SMEM),
            pl.BlockSpec((groups, part, 2) + block, lambda s: (0, s, 0, 0, 0)),
            pl.BlockSpec((groups, 2, 2) + block, lambda s: (0, 0, 0, 0, 0)),
        ],
        out_specs=pl.BlockSpec((part, 2) + block, lambda s: (s, 0, 0, 0)),
        out_shape=jax.ShapeDtypeStruct((rows, 2) + block, F32),
        scratch_shapes=[pltpu.VMEM((groups, 4 * BLOCK, 4 * BLOCK), BF16)],
        compiler_params=pltpu.CompilerParams(vmem_limit_bytes=32 * 1024 * 1024),
        name="product_terms",
    )(pattern, a_all, p_all)


def sum_kernel(copies, in_ref, out_ref):
    total = in_ref[0]
    for s in range(1, in_ref.shape[0]):
        total = total + in_ref[s]
    rounded = total.astype(BF16)
    for c in range(copies):
        out_ref[c] = rounded


def coarse_kernel(left_ref, prod_ref, out_ref):
    groups = left_ref.shape[0]
    total = jnp.zeros((groups * BLOCK, 4 * BLOCK), F32)
    for i in range(0, prod_ref.shape[0], 2):
        left = jnp.concatenate(
            [
                left_ref[:, (i + e) // 8, (i + e) % 8].reshape(groups * BLOCK, 2 * BLOCK)
                for e in range(2)
            ],
            axis=1,
        )
        right = jnp.concatenate(
            [real_pair([prod_ref[i + e, 0], prod_ref[i + e, 1]]) for e in range(2)], axis=0
        )
        total = total + jnp.dot(left, right, preferred_element_type=F32)
    for b in range(2):
        out_ref[:, b] = (
            total[:, b * 2 * BLOCK : (b + 1) * 2 * BLOCK]
            .reshape(groups, BLOCK, 2 * BLOCK)
            .astype(BF16)
        )


def final_kernel(in_ref, out_ref):
    total = in_ref[0].astype(F32)
    for s in range(1, in_ref.shape[0]):
        total = total + in_ref[s].astype(F32)
    out_ref[0] = total


def call(kernel, out_shape, *args):
    return pl.pallas_call(
        kernel,
        out_shape=out_shape,
        in_specs=[pl.BlockSpec(memory_space=pltpu.VMEM)] * len(args),
        out_specs=pl.BlockSpec(memory_space=pltpu.VMEM),
        compiler_params=pltpu.CompilerParams(vmem_limit_bytes=32 * 1024 * 1024),
    )(*args)


def transposed(blocks):
    lead = blocks.shape[:-2]
    split = blocks.reshape(lead + (BLOCK, 2, BLOCK))
    return jnp.swapaxes(split, -3, -1).reshape(lead + (BLOCK, 2 * BLOCK))


def per_device(a_blocks, a_pattern, p_blocks, p_pattern):
    x = lax.axis_index("rep")
    core = lax.axis_index("core")
    layers, rings = lax.axis_size("rep"), lax.axis_size("row")
    a_all = lax.all_gather(a_blocks, ("pair", "odd", "core"), axis=0, tiled=False)
    columns = 2 * lax.axis_size("pair") * lax.axis_size("odd")
    kept = lax.all_to_all(
        jnp.broadcast_to(a_pattern[None], (columns,) + a_pattern.shape), ("pair", "odd", "core"), 0, 0, tiled=True
    )
    p_live = jnp.where(p_pattern[:, :, None, None] > 0, p_blocks, jnp.zeros_like(p_blocks))

    mine = lax.dynamic_slice_in_dim(
        p_live.reshape(2, 4, 2, 2, BLOCK, 2 * BLOCK), x, 1, axis=1
    ).reshape(1, 2, 2, 2, BLOCK, 2 * BLOCK)
    met = lax.all_to_all(
        jnp.broadcast_to(mine, (rings,) + mine.shape[1:]), "row", 0, 0, tiled=True
    )

    column = lax.dynamic_index_in_dim(p_live, x % 2, axis=1, keepdims=False)
    column = transposed(column)
    other = lax.ppermute(column, "core", [(0, 1), (1, 0)])
    column = jnp.where(core == x // 2, column, other)
    beside = lax.ppermute(column, ("odd", "core"), [(0, 2), (3, 1)])
    left = lax.all_gather(
        jnp.where(lax.axis_index("odd") == core, column, beside), ("pair", "core"), axis=0, tiled=False
    ).reshape(8, 2, 8, BLOCK, 2 * BLOCK)

    terms = partial_product(kept.reshape(-1), a_all, met.reshape(2 * rings, 2, 2, BLOCK, 2 * BLOCK))
    swapped = lax.all_to_all(terms, "rep", 0, 0, tiled=True)
    share = terms.shape[0] // layers
    product = call(
        functools.partial(sum_kernel, layers),
        jax.ShapeDtypeStruct((layers, share, 2, BLOCK, 2 * BLOCK), BF16),
        swapped.reshape(layers, share, 2, BLOCK, 2 * BLOCK),
    )
    product = lax.all_to_all(product, "rep", 0, 0, tiled=True)
    coarse = call(
        coarse_kernel,
        jax.ShapeDtypeStruct((8, 2, BLOCK, 2 * BLOCK), BF16),
        left,
        product.reshape(layers * share, 2, BLOCK, 2 * BLOCK),
    )
    coarse = lax.all_to_all(coarse, "row", 0, 0, tiled=True)
    return call(final_kernel, jax.ShapeDtypeStruct((1, 2, BLOCK, 2 * BLOCK), F32), coarse)


def solution(mesh):
    rows, cols, reps = (mesh.shape[name] for name in ("row", "col", "rep"))
    shape = (rows, cols // 4, 2, 2, reps)
    fine = Mesh(mesh.devices.reshape(shape), ("row", "pair", "odd", "core", "rep"))
    return jax.shard_map(
        per_device,
        mesh=fine,
        in_specs=(
            P("row", ("pair", "odd", "core", "rep"), None, None),
            P("row", ("pair", "odd", "core", "rep")),
            P("row", ("pair", "odd", "core"), None, None),
            P("row", ("pair", "odd", "core")),
        ),
        out_specs=P(("row", "rep"), ("pair", "odd", "core"), None, None),
        check_vma=False,
    )
```

```python
import functools

import jax
import jax.numpy as jnp
from jax import lax
from jax.experimental import pallas as pl
from jax.experimental.pallas import tpu as pltpu
from jax.sharding import Mesh, PartitionSpec as P

BLOCK = 64
BF16 = jnp.bfloat16
F32 = jnp.float32


def lower_half(block):
    lane = lax.broadcasted_iota(jnp.int32, block.shape, block.ndim - 1)
    turned = jnp.concatenate([block[..., BLOCK:], block[..., :BLOCK]], axis=-1)
    return jnp.where(lane < BLOCK, -turned, turned)


def real_pair(blocks):
    return jnp.concatenate([jnp.concatenate([b, lower_half(b)], axis=0) for b in blocks], axis=1)


def product_kernel(a_ref, p_ref, out_ref, right):
    groups, part = a_ref.shape[0], a_ref.shape[1]

    @pl.when(pl.program_id(0) == 0)
    def _():
        for g in range(groups):
            right[g] = jnp.concatenate(
                [real_pair([p_ref[g, e, 0], p_ref[g, e, 1]]) for e in range(2)], axis=0
            )

    total = jnp.zeros((part * BLOCK, 4 * BLOCK), F32)
    for g in range(groups):
        left = jnp.concatenate(
            [a_ref[g, :, e].reshape(part * BLOCK, 2 * BLOCK) for e in range(2)], axis=1
        )
        total += jnp.dot(left, right[g], preferred_element_type=F32)
    for b in range(2):
        out_ref[:, b] = total[:, b * 2 * BLOCK : (b + 1) * 2 * BLOCK].reshape(part, BLOCK, 2 * BLOCK)


def partial_product(a_all, p_all, part=8):
    groups, rows = a_all.shape[0], a_all.shape[1]
    block = (BLOCK, 2 * BLOCK)
    return pl.pallas_call(
        product_kernel,
        grid=(rows // part,),
        in_specs=[
            pl.BlockSpec((groups, part, 2) + block, lambda s: (0, s, 0, 0, 0)),
            pl.BlockSpec((groups, 2, 2) + block, lambda s: (0, 0, 0, 0, 0)),
        ],
        out_specs=pl.BlockSpec((part, 2) + block, lambda s: (s, 0, 0, 0)),
        out_shape=jax.ShapeDtypeStruct((rows, 2) + block, F32),
        scratch_shapes=[pltpu.VMEM((groups, 4 * BLOCK, 4 * BLOCK), BF16)],
        compiler_params=pltpu.CompilerParams(vmem_limit_bytes=32 * 1024 * 1024),
        name="product_terms",
    )(a_all, p_all)


def sum_kernel(copies, in_ref, out_ref):
    total = in_ref[0]
    for s in range(1, in_ref.shape[0]):
        total = total + in_ref[s]
    rounded = total.astype(BF16)
    for c in range(copies):
        out_ref[c] = rounded


def coarse_kernel(left_ref, prod_ref, out_ref):
    groups = left_ref.shape[0]
    total = jnp.zeros((groups * BLOCK, 4 * BLOCK), F32)
    for i in range(0, prod_ref.shape[0], 2):
        left = jnp.concatenate(
            [
                left_ref[:, (i + e) // 8, (i + e) % 8].reshape(groups * BLOCK, 2 * BLOCK)
                for e in range(2)
            ],
            axis=1,
        )
        right = jnp.concatenate(
            [real_pair([prod_ref[i + e, 0], prod_ref[i + e, 1]]) for e in range(2)], axis=0
        )
        total = total + jnp.dot(left, right, preferred_element_type=F32)
    for b in range(2):
        out_ref[:, b] = (
            total[:, b * 2 * BLOCK : (b + 1) * 2 * BLOCK]
            .reshape(groups, BLOCK, 2 * BLOCK)
            .astype(BF16)
        )


def final_kernel(in_ref, out_ref):
    total = in_ref[0].astype(F32)
    for s in range(1, in_ref.shape[0]):
        total = total + in_ref[s].astype(F32)
    out_ref[0] = total


def call(kernel, out_shape, *args):
    return pl.pallas_call(
        kernel,
        out_shape=out_shape,
        in_specs=[pl.BlockSpec(memory_space=pltpu.VMEM)] * len(args),
        out_specs=pl.BlockSpec(memory_space=pltpu.VMEM),
        compiler_params=pltpu.CompilerParams(vmem_limit_bytes=32 * 1024 * 1024),
    )(*args)


def transposed(blocks):
    lead = blocks.shape[:-2]
    split = blocks.reshape(lead + (BLOCK, 2, BLOCK))
    return jnp.swapaxes(split, -3, -1).reshape(lead + (BLOCK, 2 * BLOCK))


def per_device(a_blocks, a_pattern, p_blocks, p_pattern):
    x = lax.axis_index("rep")
    core = lax.axis_index("core")
    layers, rings = lax.axis_size("rep"), lax.axis_size("row")
    a_live = jnp.where(a_pattern[:, :, None, None] > 0, a_blocks, jnp.zeros_like(a_blocks))
    a_all = lax.all_gather(a_live, ("pair", "odd", "core"), axis=0, tiled=False)
    p_live = jnp.where(p_pattern[:, :, None, None] > 0, p_blocks, jnp.zeros_like(p_blocks))

    mine = lax.dynamic_slice_in_dim(
        p_live.reshape(2, 4, 2, 2, BLOCK, 2 * BLOCK), x, 1, axis=1
    ).reshape(1, 2, 2, 2, BLOCK, 2 * BLOCK)
    met = lax.all_to_all(
        jnp.broadcast_to(mine, (rings,) + mine.shape[1:]), "row", 0, 0, tiled=True
    )

    column = lax.dynamic_index_in_dim(p_live, x % 2, axis=1, keepdims=False)
    column = transposed(column)
    other = lax.ppermute(column, "core", [(0, 1), (1, 0)])
    column = jnp.where(core == x // 2, column, other)
    beside = lax.ppermute(column, ("odd", "core"), [(0, 2), (3, 1)])
    left = lax.all_gather(
        jnp.where(lax.axis_index("odd") == core, column, beside), ("pair", "core"), axis=0, tiled=False
    ).reshape(8, 2, 8, BLOCK, 2 * BLOCK)

    terms = partial_product(a_all, met.reshape(2 * rings, 2, 2, BLOCK, 2 * BLOCK))
    swapped = lax.all_to_all(terms, "rep", 0, 0, tiled=True)
    share = terms.shape[0] // layers
    product = call(
        functools.partial(sum_kernel, layers),
        jax.ShapeDtypeStruct((layers, share, 2, BLOCK, 2 * BLOCK), BF16),
        swapped.reshape(layers, share, 2, BLOCK, 2 * BLOCK),
    )
    product = lax.all_to_all(product, "rep", 0, 0, tiled=True)
    coarse = call(
        coarse_kernel,
        jax.ShapeDtypeStruct((8, 2, BLOCK, 2 * BLOCK), BF16),
        left,
        product.reshape(layers * share, 2, BLOCK, 2 * BLOCK),
    )
    coarse = lax.all_to_all(coarse, "row", 0, 0, tiled=True)
    return call(final_kernel, jax.ShapeDtypeStruct((1, 2, BLOCK, 2 * BLOCK), F32), coarse)


def solution(mesh):
    rows, cols, reps = (mesh.shape[name] for name in ("row", "col", "rep"))
    shape = (rows, cols // 4, 2, 2, reps)
    fine = Mesh(mesh.devices.reshape(shape), ("row", "pair", "odd", "core", "rep"))
    return jax.shard_map(
        per_device,
        mesh=fine,
        in_specs=(
            P("row", ("pair", "odd", "core", "rep"), None, None),
            P("row", ("pair", "odd", "core", "rep")),
            P("row", ("pair", "odd", "core"), None, None),
            P("row", ("pair", "odd", "core")),
        ),
        out_specs=P(("row", "rep"), ("pair", "odd", "core"), None, None),
        check_vma=False,
    )
```

```python
import functools

import jax
import jax.numpy as jnp
from jax import lax
from jax.experimental import pallas as pl
from jax.experimental.pallas import tpu as pltpu
from jax.sharding import Mesh, PartitionSpec as P

BLOCK = 64
BF16 = jnp.bfloat16
F32 = jnp.float32


def lower_half(block):
    lane = lax.broadcasted_iota(jnp.int32, block.shape, block.ndim - 1)
    turned = jnp.concatenate([block[..., BLOCK:], block[..., :BLOCK]], axis=-1)
    return jnp.where(lane < BLOCK, -turned, turned)


def real_pair(blocks):
    return jnp.concatenate([jnp.concatenate([b, lower_half(b)], axis=0) for b in blocks], axis=1)


def product_kernel(a_ref, p_ref, out_ref, right):
    groups, part = a_ref.shape[0], a_ref.shape[1]

    @pl.when(pl.program_id(0) == 0)
    def _():
        for g in range(groups):
            right[g] = jnp.concatenate(
                [real_pair([p_ref[g, e, 0], p_ref[g, e, 1]]) for e in range(2)], axis=0
            )

    total = jnp.zeros((part * BLOCK, 4 * BLOCK), F32)
    for g in range(groups):
        left = jnp.concatenate(
            [a_ref[g, :, e].reshape(part * BLOCK, 2 * BLOCK) for e in range(2)], axis=1
        )
        total += jnp.dot(left, right[g], preferred_element_type=F32)
    for b in range(2):
        out_ref[:, b] = total[:, b * 2 * BLOCK : (b + 1) * 2 * BLOCK].reshape(part, BLOCK, 2 * BLOCK)


def partial_product(a_all, p_all, part=8):
    groups, rows = a_all.shape[0], a_all.shape[1]
    block = (BLOCK, 2 * BLOCK)
    return pl.pallas_call(
        product_kernel,
        grid=(rows // part,),
        in_specs=[
            pl.BlockSpec((groups, part, 2) + block, lambda s: (0, s, 0, 0, 0)),
            pl.BlockSpec((groups, 2, 2) + block, lambda s: (0, 0, 0, 0, 0)),
        ],
        out_specs=pl.BlockSpec((part, 2) + block, lambda s: (s, 0, 0, 0)),
        out_shape=jax.ShapeDtypeStruct((rows, 2) + block, F32),
        scratch_shapes=[pltpu.VMEM((groups, 4 * BLOCK, 4 * BLOCK), BF16)],
        compiler_params=pltpu.CompilerParams(vmem_limit_bytes=32 * 1024 * 1024),
        name="product_terms",
    )(a_all, p_all)


def sum_kernel(copies, in_ref, out_ref):
    total = in_ref[0]
    for s in range(1, in_ref.shape[0]):
        total = total + in_ref[s]
    rounded = total.astype(BF16)
    for c in range(copies):
        out_ref[c] = rounded


def coarse_kernel(left_ref, prod_ref, out_ref):
    groups = left_ref.shape[0]
    total = jnp.zeros((groups * BLOCK, 4 * BLOCK), F32)
    for i in range(0, prod_ref.shape[0], 4):
        left = jnp.concatenate(
            [
                left_ref[:, (i + e) // 8, (i + e) % 8].reshape(groups * BLOCK, 2 * BLOCK)
                for e in range(4)
            ],
            axis=1,
        )
        right = jnp.concatenate(
            [real_pair([prod_ref[i + e, 0], prod_ref[i + e, 1]]) for e in range(4)], axis=0
        )
        total = total + jnp.dot(left, right, preferred_element_type=F32)
    for b in range(2):
        out_ref[:, b] = (
            total[:, b * 2 * BLOCK : (b + 1) * 2 * BLOCK]
            .reshape(groups, BLOCK, 2 * BLOCK)
            .astype(BF16)
        )


def final_kernel(in_ref, out_ref):
    total = in_ref[0].astype(F32)
    for s in range(1, in_ref.shape[0]):
        total = total + in_ref[s].astype(F32)
    out_ref[0] = total


def call(kernel, out_shape, *args):
    return pl.pallas_call(
        kernel,
        out_shape=out_shape,
        in_specs=[pl.BlockSpec(memory_space=pltpu.VMEM)] * len(args),
        out_specs=pl.BlockSpec(memory_space=pltpu.VMEM),
        compiler_params=pltpu.CompilerParams(vmem_limit_bytes=32 * 1024 * 1024),
    )(*args)


def transposed(blocks):
    lead = blocks.shape[:-2]
    split = blocks.reshape(lead + (BLOCK, 2, BLOCK))
    return jnp.swapaxes(split, -3, -1).reshape(lead + (BLOCK, 2 * BLOCK))


def per_device(a_blocks, a_pattern, p_blocks, p_pattern):
    x = lax.axis_index("rep")
    core = lax.axis_index("core")
    layers, rings = lax.axis_size("rep"), lax.axis_size("row")
    a_live = jnp.where(a_pattern[:, :, None, None] > 0, a_blocks, jnp.zeros_like(a_blocks))
    a_all = lax.all_gather(a_live, ("pair", "odd", "core"), axis=0, tiled=False)
    p_live = jnp.where(p_pattern[:, :, None, None] > 0, p_blocks, jnp.zeros_like(p_blocks))

    mine = lax.dynamic_slice_in_dim(
        p_live.reshape(2, 4, 2, 2, BLOCK, 2 * BLOCK), x, 1, axis=1
    ).reshape(1, 2, 2, 2, BLOCK, 2 * BLOCK)
    met = lax.all_to_all(
        jnp.broadcast_to(mine, (rings,) + mine.shape[1:]), "row", 0, 0, tiled=True
    )

    column = lax.dynamic_index_in_dim(p_live, x % 2, axis=1, keepdims=False)
    column = transposed(column)
    other = lax.ppermute(column, "core", [(0, 1), (1, 0)])
    column = jnp.where(core == x // 2, column, other)
    beside = lax.ppermute(column, ("odd", "core"), [(0, 2), (3, 1)])
    left = lax.all_gather(
        jnp.where(lax.axis_index("odd") == core, column, beside), ("pair", "core"), axis=0, tiled=False
    ).reshape(8, 2, 8, BLOCK, 2 * BLOCK)

    terms = partial_product(a_all, met.reshape(2 * rings, 2, 2, BLOCK, 2 * BLOCK))
    swapped = lax.all_to_all(terms, "rep", 0, 0, tiled=True)
    share = terms.shape[0] // layers
    product = call(
        functools.partial(sum_kernel, layers),
        jax.ShapeDtypeStruct((layers, share, 2, BLOCK, 2 * BLOCK), BF16),
        swapped.reshape(layers, share, 2, BLOCK, 2 * BLOCK),
    )
    product = lax.all_to_all(product, "rep", 0, 0, tiled=True)
    coarse = call(
        coarse_kernel,
        jax.ShapeDtypeStruct((8, 2, BLOCK, 2 * BLOCK), BF16),
        left,
        product.reshape(layers * share, 2, BLOCK, 2 * BLOCK),
    )
    coarse = lax.all_to_all(coarse, "row", 0, 0, tiled=True)
    return call(final_kernel, jax.ShapeDtypeStruct((1, 2, BLOCK, 2 * BLOCK), F32), coarse)


def solution(mesh):
    rows, cols, reps = (mesh.shape[name] for name in ("row", "col", "rep"))
    shape = (rows, cols // 4, 2, 2, reps)
    fine = Mesh(mesh.devices.reshape(shape), ("row", "pair", "odd", "core", "rep"))
    return jax.shard_map(
        per_device,
        mesh=fine,
        in_specs=(
            P("row", ("pair", "odd", "core", "rep"), None, None),
            P("row", ("pair", "odd", "core", "rep")),
            P("row", ("pair", "odd", "core"), None, None),
            P("row", ("pair", "odd", "core")),
        ),
        out_specs=P(("row", "rep"), ("pair", "odd", "core"), None, None),
        check_vma=False,
    )
```
